32 devices in a mesh: group: 4 (over x, core), inner: 8 (over z, y).
Axes of the slice: x: 2, y: 2, z: 4, core: 2. Of those that a mesh axis runs over, the one named last changes fastest.
Arguments:
- flow_field: float32 [1536, 1536, 128], P('inner', 'group'), may hold values from -6 to 6
- sketch_rows: float32 [1536, 128], P('inner'), may hold values from -6 to 6
- sketch_cols: float32 [1536, 128], P('group'), may hold values from -6 to 6
- sketch_depth: float32 [128, 128], replicated, may hold values from -6 to 6
- bit_widths: int32 [2], replicated, may hold values from 6 to 8
- bin_edges: int32 [9], replicated, may hold values from -6 to 6, as said below
Outputs:
- basis_one: float32 [1536, 128], P('inner')
- basis_two: float32 [1536, 128], P('group')
- core: float32 [128, 128, 128], P('inner', 'group')
- residual: float32 [2, 128, 128, 128], P(None, 'inner', 'group')
- energy: float32 [2, 1536, 128], P(None, 'inner')
- histogram: float32 [2, 1536, 8], P(None, 'inner')
The draws below stay inside these ranges and needn't reach their ends.
Inputs may be any that keep to these rules, and one draw needn't show every extreme that they name: `bin_edges`: strictly increasing; the first is -6 and the last 6.
All inputs are finite; a program needn't handle non-finite values.
Results may differ from the reference program's by a relative error of at most 0.0008.
Values sent between devices are 32-bit elements; how exact they have to be, the bound alone decides.
A program may use at most 128 MiB of HBM per device.

```python
import jax
import jax.numpy as jnp
from jax import lax

N1 = 1536
N2 = 1536
N3 = 128
R = 128
NB = 2
NEDGE = 9
EDGE_SPAN = 6
NBINS = 8


def draw_bin_edges(key, part):
    candidates = jax.random.permutation(key, 2 * EDGE_SPAN - 1)[:NEDGE - 2]
    middle_edges = jnp.sort(candidates).astype(jnp.int32) - (EDGE_SPAN - 1)
    low_end = jnp.full((1,), -EDGE_SPAN, jnp.int32)
    high_end = jnp.full((1,), EDGE_SPAN, jnp.int32)
    return jnp.concatenate([low_end, middle_edges, high_end]).astype(jnp.int32)


def level_of(key, dims, split, low, largest):
    level = 1.0
    for axis_at, shards_of in split:
        steps = jax.random.uniform(jax.random.fold_in(jax.random.fold_in(key, 6), axis_at), (shards_of,), jnp.float32, low / len(split), largest / len(split))
        level = level * jnp.repeat(jnp.exp(steps), dims[axis_at] // shards_of).reshape((-1,) + (1,) * (len(dims) - 1 - axis_at))
    return level


def noise(rng, shape, deviation, limit, cuts=(), dtype=jnp.bfloat16):
    drawn = deviation * jax.random.normal(rng, shape, jnp.float32)
    if cuts:
        drawn = drawn * level_of(rng, shape, cuts, -0.22, 0.18)
    return jnp.clip(drawn, -limit, limit).astype(dtype)


def setup_inputs(seed: int = 0) -> dict:
    arg_keys = jax.random.split(jax.random.key(seed), 7)
    return {
        "flow_field": noise(arg_keys[0], (N1, N2, N3), 1.0, 6.0, ((0, 8), (1, 4)), jnp.float32),
        "sketch_rows": noise(arg_keys[1], (N1, R), 1.0, 6.0, ((0, 8),), jnp.float32),
        "sketch_cols": noise(arg_keys[2], (N2, R), 1.0, 6.0, ((0, 4),), jnp.float32),
        "sketch_depth": noise(arg_keys[3], (N3, R), 1.0, 6.0, (), jnp.float32),
        "bit_widths": jax.random.randint(arg_keys[4], (NB,), 6, 9).astype(jnp.int32),
        "bin_edges": draw_bin_edges(jax.random.fold_in(arg_keys[6], 71), 0),
    }


precise = lax.Precision.HIGHEST
two_pi = 2.0 * 3.141592653589793
error_boost = 16.0
row_block = 32

def orthonormal(sketch):
    gram_matrix = jnp.dot(sketch.T, sketch, precision=precise)
    lower_factor = jnp.linalg.cholesky(gram_matrix)
    return jax.scipy.linalg.solve_triangular(lower_factor, sketch.T, lower=True).T

def reference(flow_field, sketch_rows, sketch_cols, sketch_depth, bit_widths, bin_edges):

    def row_step(running, inputs):
        field_row, weight = inputs
        reduced = jnp.dot(field_row, sketch_depth, precision=precise)
        first_mode = jnp.sum(reduced * sketch_cols, axis=0)
        return (running + reduced * weight[None, :], first_mode)
    mode_two, mode_one = lax.scan(row_step, jnp.zeros((N2, R), jnp.float32), (flow_field, sketch_rows))
    basis_one = orthonormal(mode_one)
    basis_two = orthonormal(mode_two)
    along_two = jnp.einsum('ijk,js->isk', flow_field, basis_two, precision=precise)
    core_values = jnp.einsum('ir,isk->rsk', basis_one, along_two, precision=precise)
    peak = jnp.max(jnp.abs(core_values))
    levels = jnp.exp2(bit_widths.astype(jnp.float32) - 1.0) - 1.0
    step_size = peak / levels
    residual = -jnp.sin(two_pi * core_values[None] / step_size[:, None, None, None]) / two_pi
    error_scale = error_boost * (N1 * N2) ** 0.5 / R
    edge_values = bin_edges.astype(jnp.float32)
    blocks = basis_one.reshape(N1 // row_block, row_block, R)

    def block_stats(block_basis):
        mixed_core = jnp.einsum('ir,brsk->bisk', block_basis, residual, precision=precise)
        field_error = error_scale * jnp.einsum('bisk,js->bijk', mixed_core, basis_two, precision=precise)
        energy_part = jnp.sum(field_error * field_error, axis=2) / N2
        ramp_sums = jnp.stack([jnp.sum(jnp.clip(field_error - edge_values[index_edge] + 0.5, 0.0, 1.0), axis=(2, 3)) for index_edge in range(NEDGE)], axis=-1)
        return (energy_part, ramp_sums)
    energy_blocks, ramp_blocks = lax.map(block_stats, blocks)
    energy = jnp.transpose(energy_blocks, (1, 0, 2, 3)).reshape(NB, N1, N3)
    ramp_sums = jnp.transpose(ramp_blocks, (1, 0, 2, 3)).reshape(NB, N1, NEDGE)
    histogram = (ramp_sums[..., :-1] - ramp_sums[..., 1:]) * (NBINS / (N2 * N3))
    return (basis_one, basis_two, core_values, residual, energy, histogram)
```

```python
import functools
import math

import jax
import jax.numpy as jnp
from jax import lax
from jax.experimental import pallas as pl
from jax.experimental.pallas import tpu as pltpu
from jax.sharding import PartitionSpec as P

NEDGE = 9
NBINS = 8

precise = lax.Precision.HIGHEST
error_boost = 16.0
two_pi = 2.0 * math.pi
sine_terms = [
    (-1.0) ** n * two_pi ** (2 * n) / math.factorial(2 * n + 1) for n in range(7)
]


def soft_residual(core_values, inverse_step):
    turns = core_values * inverse_step
    turns = turns - jnp.round(turns)
    size = jnp.abs(turns)
    folded = jnp.where(size > 0.25, 0.5 - size, size)
    folded = jnp.where(turns < 0.0, folded, -folded)
    square = folded * folded
    value = jnp.full_like(square, sine_terms[-1])
    for term in sine_terms[-2::-1]:
        value = value * square + term
    return folded * value


def error_kernel(low_ref, basis_ref, mixed_ref, out_ref, *, chunk):
    rows = mixed_ref.shape[1]
    depth = mixed_ref.shape[3]
    cells = basis_ref.shape[0]

    def one_row(i, carry):
        wide = jnp.concatenate([mixed_ref[0, i], mixed_ref[1, i]], axis=1)
        high = wide.astype(jnp.bfloat16)
        rest = (wide - high.astype(jnp.float32)).astype(jnp.bfloat16)
        both = jnp.concatenate([high, rest], axis=0)
        sums = [[None] * (NEDGE + 1) for _ in range(2)]
        for start in range(0, cells, chunk):
            error = jnp.dot(
                basis_ref[start : start + chunk, :], both, preferred_element_type=jnp.float32
            )
            for b in range(2):
                part = error[:, b * depth : (b + 1) * depth].reshape(chunk // 8, 8, depth)
                pieces = [
                    jnp.sum(
                        jnp.minimum(jnp.maximum(part, low_ref[e]), low_ref[e] + 1.0), axis=0
                    )
                    for e in range(NEDGE)
                ]
                pieces.append(jnp.sum(part * part, axis=0))
                sums[b] = [p if s is None else s + p for s, p in zip(sums[b], pieces)]
        for b in range(2):
            for e in range(NEDGE):
                shifted = sums[b][e] - (cells // 8) * low_ref[e]
                out_ref[b, i, e : e + 1, :] = jnp.sum(shifted, axis=0, keepdims=True)
            out_ref[b, i, NEDGE : NEDGE + 1, :] = jnp.sum(sums[b][NEDGE], axis=0, keepdims=True)
        return carry

    lax.fori_loop(0, rows, one_row, 0)


def error_sums(low_edges, basis, mixed):
    rows, ranks, depth = mixed.shape[1:]
    cells = basis.shape[0]
    block = math.gcd(rows, 16)
    chunk = math.gcd(cells, 128)
    return pl.pallas_call(
        functools.partial(error_kernel, chunk=chunk),
        grid=(rows // block,),
        in_specs=[
            pl.BlockSpec(memory_space=pltpu.SMEM),
            pl.BlockSpec((cells, 2 * ranks), lambda i: (0, 0)),
            pl.BlockSpec((2, block, ranks, depth), lambda i: (0, i, 0, 0)),
        ],
        out_specs=pl.BlockSpec((2, block, NEDGE + 1, depth), lambda i: (0, i, 0, 0)),
        out_shape=jax.ShapeDtypeStruct((2, rows, NEDGE + 1, depth), jnp.float32),
        compiler_params=pltpu.CompilerParams(vmem_limit_bytes=32 * 1024 * 1024),
    )(low_edges, jnp.concatenate([basis, basis], axis=1), mixed)


def gram_of(sketch):
    return jnp.dot(sketch.T, sketch, precision=precise)


def local(groups, inners, flow_field, sketch_rows, sketch_cols, sketch_depth, bit_widths, bin_edges):
    ranks = sketch_depth.shape[1]
    depth = flow_field.shape[2]
    n1 = flow_field.shape[0] * inners
    n2 = flow_field.shape[1] * groups
    reduced = jnp.einsum("ijk,kr->ijr", flow_field, sketch_depth, precision=precise)
    mode_one = jnp.einsum("ijr,jr->ir", reduced, sketch_cols, precision=precise)
    mode_two = jnp.einsum("ijr,ir->jr", reduced, sketch_rows, precision=precise)
    mode_one = lax.psum(mode_one, "group")
    mode_two = lax.psum(mode_two, "inner")
    gram_one = lax.psum(gram_of(mode_one), "inner")
    gram_two = lax.psum(gram_of(mode_two), "group")
    lower = jnp.linalg.cholesky(jnp.stack([gram_one, gram_two]))
    unit = jnp.broadcast_to(jnp.eye(ranks, dtype=jnp.float32), lower.shape)
    inverse = jax.scipy.linalg.solve_triangular(lower, unit, lower=True)
    basis_one = jnp.einsum("ir,sr->is", mode_one, inverse[0], precision=precise)
    basis_two = jnp.einsum("jr,sr->js", mode_two, inverse[1], precision=precise)
    along_two = jnp.einsum("ijk,js->isk", flow_field, basis_two, precision=precise)
    partial_core = jnp.einsum("ir,isk->rsk", basis_one, along_two, precision=precise)
    partial_core = lax.psum_scatter(partial_core, "group", scatter_dimension=1, tiled=True)
    core_shard = lax.psum_scatter(partial_core, "inner", scatter_dimension=0, tiled=True)
    spread = lax.all_gather(core_shard, "inner", axis=0, tiled=True)
    core = lax.all_gather(spread, "group", axis=1, tiled=True)
    peak = jnp.max(jnp.abs(core))
    levels = jnp.exp2(bit_widths.astype(jnp.float32) - 1.0) - 1.0
    inverse_step = levels / peak
    residual_shard = soft_residual(core_shard[None], inverse_step[:, None, None, None])
    residual = soft_residual(core[None], inverse_step[:, None, None, None])
    mixed = jnp.einsum("ir,brsk->bisk", basis_one, residual, precision=lax.Precision.HIGH)
    error_scale = error_boost * math.sqrt(n1 * n2) / ranks
    sums = error_sums(
        bin_edges.astype(jnp.float32) - 0.5, (error_scale * basis_two).astype(jnp.bfloat16), mixed
    )
    parts = jnp.concatenate(
        [sums[:, :, NEDGE], jnp.sum(sums[:, :, :NEDGE], axis=-1)], axis=-1
    )
    total = lax.psum(parts, "group")
    energy = total[..., :depth] / n2
    ramps = total[..., depth:]
    histogram = (ramps[..., :-1] - ramps[..., 1:]) * (NBINS / (n2 * depth))
    return (basis_one, basis_two, core_shard, residual_shard, energy, histogram)


def solution(mesh):
    in_specs = (P("inner", "group", None), P("inner", None), P("group", None), P(), P(), P())
    out_specs = (
        P("inner", None),
        P("group", None),
        P("inner", "group", None),
        P(None, "inner", "group", None),
        P(None, "inner", None),
        P(None, "inner", None),
    )
    body = functools.partial(local, mesh.shape["group"], mesh.shape["inner"])
    return jax.shard_map(body, mesh=mesh, in_specs=in_specs, out_specs=out_specs, check_vma=False)
```
